1024 devices in a mesh: vpair: 128 (over y, z, core), opair: 8 (over x).
Axes of the slice: x: 8, y: 8, z: 8, core: 2. Of those that a mesh axis runs over, the one named last changes fastest.
Arguments:
- amplitudes: bfloat16 [256, 512, 512], P('opair', 'vpair'), may hold values from -6 to 6
- integrals: bfloat16 [192, 32, 512, 512], P('opair', None, 'vpair'), may hold values from -0.3125 to 0.3125
- pair_list: int32 [256, 2], replicated, may hold values from 0 to 199, as said below
- slab_tiles: int32 [192], replicated, may hold values from 0 to 8191, as said below
- occ_irrep: int32 [200], replicated, may hold values from 0 to 7
- vir_irrep: int32 [512], replicated, may hold values from 0 to 7
- occ_energy: float32 [200], replicated, may hold values from -2 to -0.5
- vir_energy: float32 [512], replicated, may hold values from 0.1 to 2.5
Outputs:
- ladder: bfloat16 [256, 512, 512], P('opair', 'vpair')
The draws below stay inside these ranges and needn't reach their ends.
Inputs may be any that keep to these rules, and one draw needn't show every extreme that they name: `pair_list`: each row is an ordered pair of distinct occupied orbitals; all rows differ, and for each row (i, j) the row (j, i) is present. `slab_tiles`: the tile ids are distinct. The owner of tile t is the index of vpair that holds virtual t // 16 among its 4; no owner has more than 3 tiles of the slab, and one owner has exactly 3.
All inputs are finite; a program needn't handle non-finite values.
Results may differ from the reference program's by a relative error of at most 0.0051.
Values may be sent and summed in bfloat16 or wider, within the bound.
A program may use at most 32 MiB of HBM per device.

```python
import jax
import jax.numpy as jnp
from jax import lax

NV = 512
NO = 200
DT = 32
OP = 256
SLAB_T = 192
A_DEV = 4
NDB = 16
MOST = 3
N_VPAIR = 128


def draw_pair_list(key, part):
    key = jax.random.fold_in(key, 11)
    key_codes = jax.random.fold_in(key, 1)
    key_shuffle = jax.random.fold_in(key, 2)
    half_count = OP // 2
    distances = NO // 2 - 1
    pair_codes = jax.random.permutation(key_codes, NO * distances)[:half_count]
    first_occ = pair_codes // distances
    second_occ = (first_occ + 1 + pair_codes % distances) % NO
    forward = jnp.stack([first_occ, second_occ], axis=1)
    backward = jnp.stack([second_occ, first_occ], axis=1)
    pairs = jnp.concatenate([forward, backward], axis=0)
    shuffle = jax.random.permutation(key_shuffle, OP)
    return pairs[shuffle].astype(jnp.int32)


def draw_slab_tiles(key, part):
    key = jax.random.fold_in(key, 17)
    key_owners = jax.random.fold_in(key, 1)
    key_offsets = jax.random.fold_in(key, 2)
    key_shuffle = jax.random.fold_in(key, 3)
    owner_perm = jax.random.permutation(key_owners, N_VPAIR)
    remaining = SLAB_T - MOST
    ranks = jnp.arange(remaining)
    owner_rest = owner_perm[1 + ranks % (N_VPAIR - 1)]
    slot_rest = ranks // (N_VPAIR - 1)
    owners = jnp.concatenate([jnp.full((MOST,), owner_perm[0]), owner_rest])
    slots = jnp.concatenate([jnp.arange(MOST), slot_rest])
    per_owner = A_DEV * NDB
    offsets = jax.random.randint(key_offsets, (N_VPAIR,), 0, per_owner)
    local_tile = (slots + offsets[owners]) % per_owner
    c_index = owners * A_DEV + local_tile // NDB
    tile_ids = c_index * NDB + local_tile % NDB
    shuffle = jax.random.permutation(key_shuffle, SLAB_T)
    return tile_ids[shuffle].astype(jnp.int32)


def touch_ends(array, key, smallest, largest):
    place = [jax.random.randint(jax.random.fold_in(key, axis), (), 0, length) for axis, length in enumerate(array.shape)]
    longest = array.shape.index(max(array.shape))
    beside = place[:longest] + [(place[longest] + 1) % array.shape[longest]] + place[longest + 1:]
    return array.at[tuple(place)].set(smallest).at[tuple(beside)].set(largest)


def block_levels(stream_key, shape, pieces, smallest, high):
    gain, own = 1.0, jax.random.fold_in(stream_key, 6)
    for axis_at, shards_of in pieces:
        heights = jnp.exp(jax.random.uniform(jax.random.fold_in(own, axis_at), (shards_of,), jnp.float32, smallest / len(pieces), high / len(pieces)))
        gain = gain * jnp.repeat(heights, shape[axis_at] // shards_of).reshape([-1 if axis == axis_at else 1 for axis in range(len(shape))])
    return gain


def bell_draw(own_key, dims, deviation, most, pieces=(), kind=jnp.bfloat16):
    values = jax.random.normal(own_key, dims, jnp.float32) * deviation
    if len(pieces) > 0:
        values = block_levels(own_key, dims, pieces, -0.22, 0.18) * values
    return jnp.clip(values, min=-most, max=most).astype(kind)


def setup_inputs(seed: int = 0) -> dict:
    arg_keys = jax.random.split(jax.random.key(seed), 9)
    amplitudes = bell_draw(arg_keys[0], (OP, NV, NV), 1.0, 6.0, ((0, 8), (1, 128)))
    integrals = bell_draw(arg_keys[1], (SLAB_T, DT, NV, NV), (SLAB_T * DT // 16) ** -0.5, 0.3125, ((0, 8), (2, 128)))
    pair_list = draw_pair_list(jax.random.fold_in(arg_keys[8], 71), 0)
    slab_tiles = draw_slab_tiles(jax.random.fold_in(arg_keys[8], 71), 0)
    occ_irrep = touch_ends(jax.random.randint(arg_keys[4], (NO,), 0, 8), jax.random.fold_in(arg_keys[4], 1), 0, 7).astype(jnp.int32)
    vir_irrep = touch_ends(jax.random.randint(arg_keys[5], (NV,), 0, 8), jax.random.fold_in(arg_keys[5], 1), 0, 7).astype(jnp.int32)
    occ_energy = jnp.clip(jax.random.uniform(arg_keys[6], (NO,), jnp.float32, -2.0, -0.5), -2.0, -0.5)
    vir_energy = jnp.clip(jax.random.uniform(arg_keys[7], (NV,), jnp.float32, 0.1, 2.5), 0.1, 2.5)
    return {"amplitudes": amplitudes, "integrals": integrals, "pair_list": pair_list, "slab_tiles": slab_tiles, "occ_irrep": occ_irrep, "vir_irrep": vir_irrep, "occ_energy": occ_energy, "vir_energy": vir_energy}


def reference(amplitudes, integrals, pair_list, slab_tiles, occ_irrep, vir_irrep, occ_energy, vir_energy):
    first_occ = pair_list[:, 0]
    second_occ = pair_list[:, 1]
    mirror_hot = (first_occ[None, :] == second_occ[:, None]) & (second_occ[None, :] == first_occ[:, None])
    mirror = jnp.sum(jnp.where(mirror_hot, jnp.arange(OP, dtype=jnp.int32)[None, :], 0), axis=1).astype(jnp.int32)
    c_index = (slab_tiles // NDB).astype(jnp.int32)
    d_index = (((slab_tiles % NDB) * DT)[:, None] + jnp.arange(DT, dtype=jnp.int32)[None, :]).astype(jnp.int32)
    direct = amplitudes[:, c_index[:, None], d_index]
    mirrored = amplitudes[mirror[:, None, None], d_index[None], c_index[None, :, None]]
    pair_sym = jnp.bitwise_xor(occ_irrep[first_occ], occ_irrep[second_occ])
    tile_sym = jnp.bitwise_xor(vir_irrep[c_index][:, None], vir_irrep[d_index])
    allowed = pair_sym[:, None, None] == tile_sym[None]
    summed = direct.astype(jnp.float32) + mirrored.astype(jnp.float32)
    sym_amp = jnp.where(allowed, summed, jnp.float32(0.0)).astype(jnp.bfloat16)
    sym_rows = sym_amp.reshape(OP, SLAB_T * DT).astype(jnp.float32)

    def a_block(block_index):
        piece = lax.dynamic_slice_in_dim(integrals, block_index * 16, 16, 2)
        piece = piece.reshape(SLAB_T * DT, 16 * NV).astype(jnp.float32)
        return jnp.dot(sym_rows, piece, precision=lax.Precision.HIGHEST).reshape(OP, 16, NV)

    blocks = lax.map(a_block, jnp.arange(NV // 16, dtype=jnp.int32))
    partial_sum = jnp.transpose(blocks, (1, 0, 2, 3)).reshape(OP, NV, NV)
    pair_energy = occ_energy[first_occ] + occ_energy[second_occ]
    denominator = pair_energy[:, None, None] - vir_energy[None, :, None] - vir_energy[None, None, :]
    return (partial_sum / denominator).astype(jnp.bfloat16)
```

```python
import jax
import jax.numpy as jnp
from jax import lax
from jax.experimental import pallas as pl
from jax.experimental.pallas import tpu as pltpu
from jax.sharding import PartitionSpec as P

MESH = pl.DeviceIdType.MESH
BF = jnp.bfloat16
F32 = jnp.float32
I32 = jnp.int32
N = 8
PAIRS, ROWS, PIECE = 256, 32, 16
TILES, PART, WIDTH = 192, 24, 32
A_DEV, VIRT = 4, 512
DEPTH = PART * WIDTH
COLS = A_DEV * VIRT


def iota(shape, axis):
    return lax.broadcasted_iota(I32, shape, axis)


def hot(mask):
    return jnp.where(mask, 1.0, 0.0).astype(BF)


def dot(a, b):
    return jnp.dot(a, b, preferred_element_type=F32)


def own_slots(tiles, owner):
    place = iota((1, TILES), 1).astype(F32)
    held = (tiles >> 6) == owner
    found, last = [], None
    for _ in range(3):
        open_ = held if last is None else held & (place > last)
        last = jnp.min(jnp.where(open_, place, 999.0), axis=1, keepdims=True)
        found.append(last)
    return found


def by_slot(values, shape, axis):
    slot = iota(shape, axis) >> 5
    return jnp.where(slot == 0, values[0], jnp.where(slot == 1, values[1], values[2]))


def kernel(
    amp, integ, slab, pairs, virr, oirr, out,
    vraw, vr, xs, xa, perm, spread, psb, tsym, xown, xoth, zs, zr, ys, yr, sy, pf, rs, rr,
    vsem, xsem, csem, zsem, ysem, gsem, hsem, rsem,
):
    v = lax.axis_index("vpair")
    x = lax.axis_index("opair")
    y, z, c = v // 16, (v // 2) % N, v % 2

    def at_x(d):
        return {"vpair": v, "opair": (x + d) % N}

    def at_y(d):
        return {"vpair": (((y + d) % N) * N + z) * 2 + c, "opair": x}

    def at_z(d):
        return {"vpair": (y * N + (z + d) % N) * 2 + c, "opair": x}

    other = {"vpair": (y * N + z) * 2 + (1 - c), "opair": x}
    steps = range(1, N)
    pending = []

    def send(src, dst, sems, i, device):
        copy = pltpu.make_async_remote_copy(
            src_ref=src, dst_ref=dst, send_sem=sems.at[0, i], recv_sem=sems.at[1, i],
            device_id=device, device_id_type=MESH,
        )
        copy.start()
        pending.append(copy)
        return copy

    load = pltpu.make_async_copy(integ, vraw, vsem)
    load.start()
    barrier = pltpu.get_barrier_semaphore()
    for device in [f(d) for f in (at_x, at_y, at_z) for d in steps] + [other]:
        pl.semaphore_signal(barrier, inc=1, device_id=device, device_id_type=MESH)

    tiles = slab[...]
    c_of, d_of = tiles >> 4, tiles & 15
    pick = hot(iota((VIRT, TILES), 0) == jnp.where(d_of == v // 8, c_of, -1))
    found = own_slots(tiles, v)
    place = iota((1, TILES), 1).astype(F32)
    ids = [
        jnp.sum(jnp.where(place == k, tiles.astype(F32), 0.0), axis=1, keepdims=True) for k in found
    ]
    tile = by_slot(ids, (1, 128), 1).astype(I32)
    wide = iota((1, 128), 1) & 31
    pick_own = hot(iota((VIRT, 128), 0) == (tile & 15) * WIDTH + wide)
    block = amp[...].reshape(ROWS * A_DEV, VIRT)
    lane = iota((1, N * 128), 1)
    target = jnp.where((lane & 31) < PART, (lane >> 7) * PART + (lane & 31), -1)
    place_in = hot(iota((TILES, N * 128), 0) == target)
    row = iota((ROWS * A_DEV, 1), 0) & 3
    columns = dot(dot(block, pick).astype(BF), place_in)
    columns = jnp.where(row == ((lane >> 5) & 3), columns, 0.0).astype(BF)
    held = jnp.where(row == ((tile >> 4) & 3), dot(block, pick_own), 0.0).astype(BF)
    fold = hot((iota((ROWS, ROWS * A_DEV), 1) >> 2) == iota((ROWS, ROWS * A_DEV), 0))
    columns = dot(fold, columns).astype(BF)
    held = dot(fold, held).astype(BF)
    for o in range(N):
        xs[o, :, 0:128] = held
        xs[o, :, 128:256] = columns[:, o * 128 : (o + 1) * 128]
    pl.semaphore_wait(barrier, 3 * (N - 1) + 1)

    to_x = [send(xs.at[(x + d) % N], xa.at[x], xsem, d, at_x(d)) for d in steps]
    xa[pl.ds(x, 1)] = xs[pl.ds(x, 1)]

    lists = pairs[...]
    first, second = lists[0:1, :], lists[1:2, :]
    code = first * 256 + second
    swapped = jnp.broadcast_to((second * 256 + first).astype(F32), (PAIRS, PAIRS)).T
    perm[...] = hot(swapped == code.astype(F32))
    part_lane = iota((1, DEPTH), 1)
    for h in range(2):
        holder = (y * N + z) * 2 + h
        slots = [k - (x * PART).astype(F32) for k in own_slots(tiles, holder)]
        r = iota((128, 1), 0)
        slot_at = by_slot(slots, (128, 1), 0).astype(I32)
        slot_at = jnp.where(r < 96, slot_at, -1)
        spread[h, 0:128] = hot(
            (slot_at == (part_lane >> 5)) & ((r & 31) == (part_lane & 31))
        )
        spread[h, 128:256] = hot(
            ((r & 31) == (part_lane >> 5))
            & ((holder % N) * A_DEV + (r >> 5) == (part_lane & 31))
        )
    irrep_hot = hot(iota((oirr.shape[1], PAIRS), 0) == first)
    irrep_hot2 = hot(iota((oirr.shape[1], PAIRS), 0) == second)
    occ = jnp.broadcast_to(oirr[...].astype(F32), (8, oirr.shape[1])).astype(BF)
    pair_sym = dot(occ, irrep_hot).astype(I32) ^ dot(occ, irrep_hot2).astype(I32)
    psb[...] = jnp.broadcast_to(pair_sym[0:1].astype(F32), (128, PAIRS)).T
    own_hot = hot(iota((TILES, DEPTH), 0) == x * PART + (part_lane >> 5))

    def own(row_values):
        wide_values = jnp.broadcast_to(row_values.astype(F32), (8, row_values.shape[1])).astype(BF)
        return dot(wide_values, own_hot)[0:1].astype(I32)

    c_row = own(c_of >> 2) * 4 + own(c_of & 3)
    d_row = own(d_of) * WIDTH + (part_lane & 31)
    vir = jnp.broadcast_to(virr[...].astype(F32), (8, VIRT)).astype(BF)
    tile_sym = [
        dot(vir, hot(iota((VIRT, DEPTH), 0) == rows))[0:1].astype(I32) for rows in (c_row, d_row)
    ]
    tsym[...] = jnp.broadcast_to((tile_sym[0] ^ tile_sym[1]).astype(F32), (8, DEPTH))

    ri, ci = iota((128, 128), 0), iota((128, 128), 1)
    regroup = hot(((ri >> 5) == (ci & 3)) & ((ri & 31) == (ci >> 2)))

    def relayout(k, _):
        rows = dot(regroup, vraw[k].reshape(WIDTH * A_DEV, VIRT)).astype(BF)
        at = pl.ds(pl.multiple_of(k * WIDTH, WIDTH), WIDTH)
        for a in range(A_DEV):
            vr[a, at, :] = rows[a * WIDTH : (a + 1) * WIDTH]
        return 0

    load.wait()
    lax.fori_loop(0, 8, relayout, 0)
    for copy in to_x:
        copy.wait_recv()

    mirrored = dot(perm[...], xa[:, :, 128:256].reshape(PAIRS, 128)).astype(BF)
    xown[:, :, 128:256] = mirrored.reshape(2, 128, 128)
    xown[:, :, 0:128] = xa[:, :, 0:128].reshape(2, 128, 128)
    to_core = send(xown.at[1 - c], xoth, csem, 0, other)
    dense = dot(xown[c], spread[c])
    to_core.wait_recv()
    dense += dot(xoth[...], spread[1 - c])
    zs[...] = dense.astype(BF).reshape(N, PIECE, DEPTH)
    to_z = [send(zs.at[(z + d) % N], zr.at[z], zsem, d, at_z(d)) for d in steps]
    zr[pl.ds(z, 1)] = zs[pl.ds(z, 1)]
    lax.fori_loop(8, 16, relayout, 0)
    for copy in to_z:
        copy.wait_recv()
    total = zr[0].astype(F32)
    for i in steps:
        total += zr[i].astype(F32)
    ys[...] = total.astype(BF)
    to_y = [send(ys, yr.at[y], ysem, d, at_y(d)) for d in steps]
    yr[pl.ds(y, 1)] = ys[...].reshape(1, PIECE, DEPTH)
    lax.fori_loop(16, 24, relayout, 0)
    for copy in to_y:
        copy.wait_recv()
    total = yr[0].astype(F32)
    for i in steps:
        total += yr[i].astype(F32)
    mine = c * N + z
    sym_of = psb[pl.ds(pl.multiple_of(mine * PIECE, PIECE), PIECE), :][:, 0:1]
    total = jnp.where(sym_of == tsym[0:1, :], total, 0.0)
    sy[pl.ds(mine, 1)] = total.astype(BF).reshape(1, PIECE, DEPTH)
    to_z = [send(sy.at[mine], sy.at[mine], gsem, d, at_z(d)) for d in steps]
    to_other = [send(sy.at[mine], sy.at[mine], hsem, 0, other)]
    for d in (1, 7, 2, 6, 3, 5, 4):
        to_z[d - 1].wait_recv()
        got = c * N + (z + N - d) % N
        to_other.append(send(sy.at[got], sy.at[got], hsem, d, other))
    for copy in to_other:
        copy.wait_recv()

    def multiply(blocks):
        rows = jnp.concatenate(
            [sy[pl.ds(((x + d) % N) * 2, 2)].reshape(ROWS, DEPTH) for d in blocks], axis=0
        )
        for a in range(A_DEV):
            sums = dot(rows, vr[a])
            for i, d in enumerate(blocks):
                pf[d, :, a * VIRT : (a + 1) * VIRT] = sums[i * ROWS : (i + 1) * ROWS]

    ring = {}

    def pass_on(way, i, got):
        distance = 4 - i if i < 4 else 7 - i
        d = distance if way == 0 else N - distance
        half = 0 if (way == 0) == (i < 4) else PIECE
        value = pf[d, half : half + PIECE, :]
        if got is not None:
            value += rr[way, got].astype(F32)
        rs[way, i] = value.astype(BF)
        ring[way, i] = send(rs.at[way, i], rr.at[way, i], rsem.at[way], i, at_x(1 if way == 0 else N - 1))

    multiply((4, 3, 5, 2))
    for i in (0, 4):
        for way in range(2):
            pass_on(way, i, None)
    multiply((6, 1, 7, 0))
    for i in (0, 4, 1, 5, 2):
        for way in range(2):
            ring[way, i].wait_recv()
            pass_on(way, i + 1, i)
    for i in (3, 6):
        for way in range(2):
            ring[way, i].wait_recv()
    halves = []
    for half, mine_, theirs in ((0, 3, 6), (PIECE, 6, 3)):
        halves.append(
            pf[0, half : half + PIECE, :] + rr[0, mine_].astype(F32) + rr[1, theirs].astype(F32)
        )
    out[0:PIECE, :] = halves[0]
    out[PIECE:ROWS, :] = halves[1]
    for copy in pending:
        copy.wait_send()


def table_lookup(indices, table):
    hits = indices[..., None] == jnp.arange(table.shape[0], dtype=jnp.int32)
    return jnp.sum(jnp.where(hits, table, jnp.zeros((), table.dtype)), axis=-1)


def local(
    amplitudes, integrals, pair_list, slab_tiles, occ_irrep, vir_irrep, occ_energy, vir_energy
):
    vp_index = lax.axis_index("vpair")
    op_index = lax.axis_index("opair")
    vmem = pl.BlockSpec(memory_space=pltpu.VMEM)
    dma = pltpu.SemaphoreType.DMA
    partial_sum = pl.pallas_call(
        kernel,
        out_shape=jax.ShapeDtypeStruct((ROWS, COLS), F32),
        in_specs=[vmem, pl.BlockSpec(memory_space=pl.ANY), vmem, vmem, vmem, vmem],
        out_specs=vmem,
        scratch_shapes=[
            pltpu.VMEM((PART, WIDTH, A_DEV, VIRT), BF),
            pltpu.VMEM((A_DEV, DEPTH, VIRT), BF),
            pltpu.VMEM((N, ROWS, 256), BF),
            pltpu.VMEM((N, ROWS, 256), BF),
            pltpu.VMEM((PAIRS, PAIRS), BF),
            pltpu.VMEM((2, 256, DEPTH), BF),
            pltpu.VMEM((PAIRS, 128), F32),
            pltpu.VMEM((8, DEPTH), F32),
            pltpu.VMEM((2, 128, 256), BF),
            pltpu.VMEM((128, 256), BF),
            pltpu.VMEM((N, PIECE, DEPTH), BF),
            pltpu.VMEM((N, PIECE, DEPTH), BF),
            pltpu.VMEM((PIECE, DEPTH), BF),
            pltpu.VMEM((N, PIECE, DEPTH), BF),
            pltpu.VMEM((2 * N, PIECE, DEPTH), BF),
            pltpu.VMEM((N, ROWS, COLS), F32),
            pltpu.VMEM((2, 7, PIECE, COLS), BF),
            pltpu.VMEM((2, 7, PIECE, COLS), BF),
            dma,
            dma((2, N)),
            dma((2, 1)),
            dma((2, N)),
            dma((2, N)),
            dma((2, N)),
            dma((2, N)),
            dma((2, 2, 7)),
        ],
        compiler_params=pltpu.CompilerParams(
            collective_id=0, has_side_effects=True, vmem_limit_bytes=60 << 20
        ),
    )(
        amplitudes,
        integrals,
        slab_tiles.reshape(1, TILES),
        pair_list.T,
        vir_irrep.reshape(1, VIRT),
        occ_irrep.reshape(1, -1),
    )
    own = lax.dynamic_slice_in_dim(pair_list, op_index * ROWS, ROWS)
    pair_energy = table_lookup(own[:, 0], occ_energy) + table_lookup(own[:, 1], occ_energy)
    own_virtual = lax.dynamic_slice_in_dim(vir_energy, vp_index * A_DEV, A_DEV)
    denominator = (
        pair_energy[:, None, None] - own_virtual[None, :, None] - vir_energy[None, None, :]
    )
    return (partial_sum.reshape(ROWS, A_DEV, VIRT) / denominator).astype(BF)


def solution(mesh):
    in_specs = (
        P("opair", "vpair", None), P("opair", None, "vpair", None), P(), P(), P(), P(), P(), P(),
    )
    out_specs = P("opair", "vpair", None)
    return jax.shard_map(local, mesh=mesh, in_specs=in_specs, out_specs=out_specs, check_vma=False)
```

```python
import jax
import jax.numpy as jnp
from jax import lax
from jax.experimental import pallas as pl
from jax.experimental.pallas import tpu as pltpu
from jax.sharding import PartitionSpec as P

MESH = pl.DeviceIdType.MESH
BF = jnp.bfloat16
F32 = jnp.float32
I32 = jnp.int32
N = 8
PAIRS, ROWS, PIECE = 256, 32, 16
TILES, PART, WIDTH = 192, 24, 32
A_DEV, VIRT = 4, 512
DEPTH = PART * WIDTH
COLS = A_DEV * VIRT
PATH = DEPTH // 2
FAR = (4, 3, 5, 2, 6, 1, 7)
NEAR = (1, 7, 2, 6, 3, 5, 4)


def iota(shape, axis):
    return lax.broadcasted_iota(I32, shape, axis)


def hot(mask):
    return jnp.where(mask, 1.0, 0.0).astype(BF)


def dot(a, b):
    return jnp.dot(a, b, preferred_element_type=F32)


def own_slots(tiles, owner):
    place = iota((1, TILES), 1).astype(F32)
    held = (tiles >> 6) == owner
    found, last = [], None
    for _ in range(3):
        open_ = held if last is None else held & (place > last)
        last = jnp.min(jnp.where(open_, place, 999.0), axis=1, keepdims=True)
        found.append(last)
    return found


def by_slot(values, shape, axis):
    slot = iota(shape, axis) >> 5
    return jnp.where(slot == 0, values[0], jnp.where(slot == 1, values[1], values[2]))


def kernel(
    amp_in, integ, slab_in, pairs_in, virr_in, oirr_in, venergy_in, oenergy_in, out,
    amp, slab, pairs, virr, oirr, venergy, oenergy,
    vraw, vr, xs, xa, perm, spread, psb, tsym, inverse, xmine, xgive, xoth,
    ps, pr, qs, qr, sy, pf, rs, rr,
    lsem, xsem, csem, psem, qsem, gsem, hsem, rsem,
):
    v = lax.axis_index("vpair")
    x = lax.axis_index("opair")
    y, z, c = v // 16, (v // 2) % N, v % 2

    def at_x(d):
        return {"vpair": v, "opair": (x + d) % N}

    def at_y(d):
        return {"vpair": (((y + d) % N) * N + z) * 2 + c, "opair": x}

    def at_z(d):
        return {"vpair": (y * N + (z + d) % N) * 2 + c, "opair": x}

    other = {"vpair": (y * N + z) * 2 + (1 - c), "opair": x}
    steps = range(1, N)
    outer, outer_at = (z, y), (at_z, at_y)
    inner, inner_at = (y, z), (at_y, at_z)
    pending = []

    def send(src, dst, sems, i, device):
        copy = pltpu.make_async_remote_copy(
            src_ref=src, dst_ref=dst, send_sem=sems.at[0, i], recv_sem=sems.at[1, i],
            device_id=device, device_id_type=MESH,
        )
        copy.start()
        pending.append(copy)
        return copy

    loads = []
    for i, (src, dst) in enumerate((
        (amp_in, amp), (slab_in, slab), (pairs_in, pairs), (virr_in, virr), (oirr_in, oirr),
        (venergy_in, venergy), (oenergy_in, oenergy), (integ, vraw),
    )):
        loads.append(pltpu.make_async_copy(src, dst, lsem.at[i]))
        loads[-1].start()
    barrier = pltpu.get_barrier_semaphore()
    for device in [f(d) for f in (at_x, at_y, at_z) for d in steps] + [other]:
        pl.semaphore_signal(barrier, inc=1, device_id=device, device_id_type=MESH)
    loads[1].wait()

    tiles = slab[...]
    c_of, d_of = tiles >> 4, tiles & 15
    pick = hot(iota((VIRT, TILES), 0) == jnp.where(d_of == v // 8, c_of, -1))
    found = own_slots(tiles, v)
    place = iota((1, TILES), 1).astype(F32)
    ids = [
        jnp.sum(jnp.where(place == k, tiles.astype(F32), 0.0), axis=1, keepdims=True) for k in found
    ]
    tile = by_slot(ids, (1, 128), 1).astype(I32)
    wide = iota((1, 128), 1) & 31
    pick_own = hot(iota((VIRT, 128), 0) == (tile & 15) * WIDTH + wide)
    loads[0].wait()
    block = amp[...].reshape(ROWS * A_DEV, VIRT)
    lane = iota((1, N * 128), 1)
    target = jnp.where((lane & 31) < PART, (lane >> 7) * PART + (lane & 31), -1)
    place_in = hot(iota((TILES, N * 128), 0) == target)
    row = iota((ROWS * A_DEV, 1), 0) & 3
    columns = dot(dot(block, pick).astype(BF), place_in)
    columns = jnp.where(row == ((lane >> 5) & 3), columns, 0.0).astype(BF)
    held = jnp.where(row == ((tile >> 4) & 3), dot(block, pick_own), 0.0).astype(BF)
    fold = hot((iota((ROWS, ROWS * A_DEV), 1) >> 2) == iota((ROWS, ROWS * A_DEV), 0))
    columns = dot(fold, columns).astype(BF)
    held = dot(fold, held).astype(BF)
    for o in range(N):
        xs[o, :, 0:128] = held
        xs[o, :, 128:256] = columns[:, o * 128 : (o + 1) * 128]
    pl.semaphore_wait(barrier, 3 * (N - 1) + 1)

    to_x = [send(xs.at[(x + d) % N], xa.at[x], xsem, d, at_x(d)) for d in FAR]
    xa[pl.ds(x, 1)] = xs[pl.ds(x, 1)]

    for i in range(2, 7):
        loads[i].wait()
    lists = pairs[...]
    first, second = lists[0:1, :], lists[1:2, :]
    code = first * 256 + second
    swapped = jnp.broadcast_to((second * 256 + first).astype(F32), (PAIRS, PAIRS)).T
    perm[...] = hot(swapped == code.astype(F32))
    part_lane = iota((1, DEPTH), 1)
    for h in range(2):
        holder = (y * N + z) * 2 + h
        slots = [k - (x * PART).astype(F32) for k in own_slots(tiles, holder)]
        r = iota((128, 1), 0)
        slot_at = by_slot(slots, (128, 1), 0).astype(I32)
        slot_at = jnp.where(r < 96, slot_at, -1)
        spread[h, 0:128] = hot(
            (slot_at == (part_lane >> 5)) & ((r & 31) == (part_lane & 31))
        )
        spread[h, 128:256] = hot(
            ((r & 31) == (part_lane >> 5))
            & ((holder % N) * A_DEV + (r >> 5) == (part_lane & 31))
        )
    irrep_hot = hot(iota((oirr.shape[1], PAIRS), 0) == first)
    irrep_hot2 = hot(iota((oirr.shape[1], PAIRS), 0) == second)
    occ = jnp.broadcast_to(oirr[...].astype(F32), (8, oirr.shape[1])).astype(BF)
    pair_sym = dot(occ, irrep_hot).astype(I32) ^ dot(occ, irrep_hot2).astype(I32)
    psb[...] = jnp.broadcast_to(pair_sym[0:1].astype(F32), (128, PAIRS)).T
    occ = jnp.broadcast_to(oenergy[...], (8, oirr.shape[1]))
    energy = sum(
        jnp.dot(
            occ, jnp.where(iota((oirr.shape[1], PAIRS), 0) == which, 1.0, 0.0),
            precision=lax.Precision.HIGHEST, preferred_element_type=F32,
        )
        for which in (first, second)
    )
    turned = jnp.broadcast_to(energy[0:1], (128, PAIRS)).T
    inverse[:, 0:128] = turned[0:ROWS]
    for o in steps:
        inverse[:, 0:128] = jnp.where(x == o, turned[o * ROWS : (o + 1) * ROWS], inverse[:, 0:128])
    pair_energy = inverse[:, 0:1]
    vir_row = venergy[...]
    vir_lane = iota((1, VIRT), 1)
    for a in range(A_DEV):
        own_virtual = jnp.sum(
            jnp.where(vir_lane == v * A_DEV + a, vir_row, 0.0), axis=1, keepdims=True
        )
        inverse[:, a * VIRT : (a + 1) * VIRT] = 1.0 / (pair_energy - own_virtual - vir_row)
    own_hot = hot(iota((TILES, DEPTH), 0) == x * PART + (part_lane >> 5))

    def own(row_values):
        wide_values = jnp.broadcast_to(row_values.astype(F32), (8, row_values.shape[1])).astype(BF)
        return dot(wide_values, own_hot)[0:1].astype(I32)

    c_row = own(c_of >> 2) * 4 + own(c_of & 3)
    d_row = own(d_of) * WIDTH + (part_lane & 31)
    vir = jnp.broadcast_to(virr[...].astype(F32), (8, VIRT)).astype(BF)
    tile_sym = [
        dot(vir, hot(iota((VIRT, DEPTH), 0) == rows))[0:1].astype(I32) for rows in (c_row, d_row)
    ]
    tsym[...] = jnp.broadcast_to((tile_sym[0] ^ tile_sym[1]).astype(F32), (8, DEPTH))

    ri, ci = iota((128, 128), 0), iota((128, 128), 1)
    regroup = hot(((ri >> 5) == (ci & 3)) & ((ri & 31) == (ci >> 2)))

    def relayout(k, _):
        rows = dot(regroup, vraw[k].reshape(WIDTH * A_DEV, VIRT)).astype(BF)
        at = pl.ds(pl.multiple_of(k * WIDTH, WIDTH), WIDTH)
        for a in range(A_DEV):
            vr[a, at, :] = rows[a * WIDTH : (a + 1) * WIDTH]
        return 0

    loads[7].wait()
    lax.fori_loop(0, 8, relayout, 0)
    for copy in to_x:
        copy.wait_recv()

    to_core = [send(xa.at[pl.ds((1 - c) * 4, 4), :, 0:128], xoth.at[0], csem, 0, other)]
    columns = xa[:, :, 128:256].reshape(PAIRS, 128)

    def mirrored(half):
        at = pl.ds(pl.multiple_of(half * 128, 128), 128)
        return dot(perm[at, :], columns).astype(BF).reshape(4, ROWS, 128)

    xgive[...] = mirrored(1 - c)
    to_core.append(send(xgive, xoth.at[1], csem, 1, other))
    xmine[0] = xa[pl.ds(c * 4, 4), :, 0:128]
    xmine[1] = mirrored(c)

    def spread_out(ref, h):
        rows = jnp.concatenate([ref[i].reshape(128, 128) for i in range(2)], axis=1)
        return dot(rows, spread[h])

    dense = spread_out(xmine, c)
    for copy in to_core:
        copy.wait_recv()
    dense += spread_out(xoth, 1 - c)
    for p in range(2):
        ps[p] = dense[:, p * PATH : (p + 1) * PATH].astype(BF).reshape(N, PIECE, PATH)
    copies = [
        send(ps.at[p, (outer[p] + d) % N], pr.at[p, outer[p]], psem.at[p], d, outer_at[p](d))
        for d in FAR for p in range(2)
    ]
    for p in range(2):
        pr[p, pl.ds(outer[p], 1)] = ps[p, pl.ds(outer[p], 1)]
    lax.fori_loop(8, 16, relayout, 0)
    for copy in copies:
        copy.wait_recv()
    for p in range(2):
        total = pr[p, 0].astype(F32)
        for i in steps:
            total += pr[p, i].astype(F32)
        qs[p] = total.astype(BF)
    copies = [
        send(qs.at[p], qr.at[p, inner[p]], qsem.at[p], d, inner_at[p](d))
        for d in FAR for p in range(2)
    ]
    for p in range(2):
        qr[p, pl.ds(inner[p], 1)] = qs[p].reshape(1, PIECE, PATH)
    lax.fori_loop(16, 24, relayout, 0)
    for copy in copies:
        copy.wait_recv()
    mine = [c * N + outer[p] for p in range(2)]
    for p in range(2):
        total = qr[p, 0].astype(F32)
        for i in steps:
            total += qr[p, i].astype(F32)
        sym_of = psb[pl.ds(pl.multiple_of(mine[p] * PIECE, PIECE), PIECE), :][:, 0:1]
        total = jnp.where(sym_of == tsym[0:1, p * PATH : (p + 1) * PATH], total, 0.0)
        sy[p, pl.ds(mine[p], 1)] = total.astype(BF).reshape(1, PIECE, PATH)
    gathered = {
        (p, d): send(sy.at[p, mine[p]], sy.at[p, mine[p]], gsem.at[p], d, outer_at[p](d))
        for d in FAR for p in range(2)
    }
    to_other = [
        send(sy.at[p, mine[p]], sy.at[p, mine[p]], hsem.at[p], 0, other) for p in range(2)
    ]
    for d in NEAR:
        for p in range(2):
            gathered[p, d].wait_recv()
            got = c * N + (outer[p] + N - d) % N
            to_other.append(send(sy.at[p, got], sy.at[p, got], hsem.at[p], d, other))
    for copy in to_other:
        copy.wait_recv()

    ring = {}

    def pass_on(way, i, q, got):
        distance = 4 - i if i < 4 else 7 - i
        d = distance if way == 0 else N - distance
        half = 0 if (way == 0) == (i < 4) else PIECE
        value = pf[d, half : half + PIECE, q * 1024 : (q + 1) * 1024]
        if got is not None:
            value += rr[way, got, q].astype(F32)
        rs[way, i, q] = value.astype(BF)
        ring[way, i, q] = send(
            rs.at[way, i, q], rr.at[way, i, q], rsem.at[way, q], i, at_x(1 if way == 0 else N - 1)
        )

    def multiply(blocks, first):
        rows = jnp.concatenate(
            [
                jnp.concatenate(
                    [sy[p, pl.ds(((x + d) % N) * 2, 2)].reshape(ROWS, PATH) for p in range(2)],
                    axis=1,
                )
                for d in blocks
            ],
            axis=0,
        )
        for a in range(A_DEV):
            sums = dot(rows, vr[a])
            for i, d in enumerate(blocks):
                pf[d, :, a * VIRT : (a + 1) * VIRT] = sums[i * ROWS : (i + 1) * ROWS]
            if first and a % 2 == 1:
                for i in (0, 4):
                    for way in range(2):
                        pass_on(way, i, a // 2, None)

    multiply((4, 3, 5, 2), True)
    multiply((6, 1, 7, 0), False)
    for i in (0, 4, 1, 5, 2):
        for q in range(2):
            for way in range(2):
                ring[way, i, q].wait_recv()
                pass_on(way, i + 1, q, i)
    for q in range(2):
        for i in (6, 3):
            for way in range(2):
                ring[way, i, q].wait_recv()
        for half, mine_, theirs in ((0, 3, 6), (PIECE, 6, 3)):
            at = (slice(half, half + PIECE), slice(q * 1024, (q + 1) * 1024))
            total = pf[0, at[0], at[1]] + rr[0, mine_, q].astype(F32) + rr[1, theirs, q].astype(F32)
            total = total * inverse[at[0], at[1]]
            for a in range(2):
                out[at[0], 2 * q + a, :] = total[:, a * VIRT : (a + 1) * VIRT].astype(out.dtype)
    for copy in pending:
        copy.wait_send()


def local(
    amplitudes, integrals, pair_list, slab_tiles, occ_irrep, vir_irrep, occ_energy, vir_energy
):
    dma = pltpu.SemaphoreType.DMA
    occupied = occ_irrep.shape[0]
    return pl.pallas_call(
        kernel,
        out_shape=jax.ShapeDtypeStruct((ROWS, A_DEV, VIRT), F32),
        in_specs=[pl.BlockSpec(memory_space=pl.ANY)] * 8,
        out_specs=pl.BlockSpec(memory_space=pltpu.VMEM),
        scratch_shapes=[
            pltpu.VMEM((ROWS, A_DEV, VIRT), BF),
            pltpu.VMEM((1, TILES), I32),
            pltpu.VMEM((2, PAIRS), I32),
            pltpu.VMEM((1, VIRT), I32),
            pltpu.VMEM((1, occupied), I32),
            pltpu.VMEM((1, VIRT), F32),
            pltpu.VMEM((1, occupied), F32),
            pltpu.VMEM((PART, WIDTH, A_DEV, VIRT), BF),
            pltpu.VMEM((A_DEV, DEPTH, VIRT), BF),
            pltpu.VMEM((N, ROWS, 256), BF),
            pltpu.VMEM((N, ROWS, 256), BF),
            pltpu.VMEM((PAIRS, PAIRS), BF),
            pltpu.VMEM((2, 256, DEPTH), BF),
            pltpu.VMEM((PAIRS, 128), F32),
            pltpu.VMEM((8, DEPTH), F32),
            pltpu.VMEM((ROWS, COLS), F32),
            pltpu.VMEM((2, 4, ROWS, 128), BF),
            pltpu.VMEM((4, ROWS, 128), BF),
            pltpu.VMEM((2, 4, ROWS, 128), BF),
            pltpu.VMEM((2, N, PIECE, PATH), BF),
            pltpu.VMEM((2, N, PIECE, PATH), BF),
            pltpu.VMEM((2, PIECE, PATH), BF),
            pltpu.VMEM((2, N, PIECE, PATH), BF),
            pltpu.VMEM((2, 2 * N, PIECE, PATH), BF),
            pltpu.VMEM((N, ROWS, COLS), F32),
            pltpu.VMEM((2, 7, 2, PIECE, 1024), BF),
            pltpu.VMEM((2, 7, 2, PIECE, 1024), BF),
            dma((8,)),
            dma((2, N)),
            dma((2, 2)),
            dma((2, 2, N)),
            dma((2, 2, N)),
            dma((2, 2, N)),
            dma((2, 2, N)),
            dma((2, 2, 2, 7)),
        ],
        compiler_params=pltpu.CompilerParams(
            collective_id=0, has_side_effects=True, vmem_limit_bytes=60 << 20
        ),
    )(
        amplitudes,
        integrals,
        slab_tiles.reshape(1, TILES),
        pair_list.T,
        vir_irrep.reshape(1, VIRT),
        occ_irrep.reshape(1, occupied),
        vir_energy.reshape(1, VIRT),
        occ_energy.reshape(1, occupied),
    ).astype(BF)


def solution(mesh):
    in_specs = (
        P("opair", "vpair", None), P("opair", None, "vpair", None), P(), P(), P(), P(), P(), P(),
    )
    out_specs = P("opair", "vpair", None)
    return jax.shard_map(local, mesh=mesh, in_specs=in_specs, out_specs=out_specs, check_vma=False)
```

```python
import jax
import jax.numpy as jnp
from jax import lax
from jax.experimental import pallas as pl
from jax.experimental.pallas import tpu as pltpu
from jax.sharding import PartitionSpec as P

MESH = pl.DeviceIdType.MESH
BF = jnp.bfloat16
F32 = jnp.float32
I32 = jnp.int32
N = 8
PAIRS, ROWS, PIECE = 256, 32, 16
TILES, PART, WIDTH = 192, 24, 32
A_DEV, VIRT = 4, 512
DEPTH = PART * WIDTH
COLS = A_DEV * VIRT
PATH = DEPTH // 2
FAR = (4, 3, 5, 2, 6, 1, 7)
NEAR = (1, 7, 2, 6, 3, 5, 4)


def iota(shape, axis):
    return lax.broadcasted_iota(I32, shape, axis)


def hot(mask):
    return jnp.where(mask, 1.0, 0.0).astype(BF)


def dot(a, b):
    return jnp.dot(a, b, preferred_element_type=F32)


def own_slots(tiles, owner):
    place = iota((1, TILES), 1).astype(F32)
    held = (tiles >> 6) == owner
    found, last = [], None
    for _ in range(3):
        open_ = held if last is None else held & (place > last)
        last = jnp.min(jnp.where(open_, place, 999.0), axis=1, keepdims=True)
        found.append(last)
    return found


def by_slot(values, shape, axis):
    slot = iota(shape, axis) >> 5
    return jnp.where(slot == 0, values[0], jnp.where(slot == 1, values[1], values[2]))


def kernel(
    amp_in, integ, slab_in, pairs_in, virr_in, oirr_in, venergy_in, oenergy_in, out,
    amp, slab, pairs, virr, oirr, venergy, oenergy,
    vraw, vr, xs, xa, perm, spread, psb, tsym, inverse, xmine, xgive, xoth,
    ps, pr, qs, qr, sy, pf, rs, rr,
    lsem, xsem, csem, psem, qsem, gsem, hsem, rsem,
):
    v = lax.axis_index("vpair")
    x = lax.axis_index("opair")
    y, z, c = v // 16, (v // 2) % N, v % 2

    def at_x(d):
        return {"vpair": v, "opair": (x + d) % N}

    def at_y(d):
        return {"vpair": (((y + d) % N) * N + z) * 2 + c, "opair": x}

    def at_z(d):
        return {"vpair": (y * N + (z + d) % N) * 2 + c, "opair": x}

    other = {"vpair": (y * N + z) * 2 + (1 - c), "opair": x}
    steps = range(1, N)
    outer, outer_at = (z, y), (at_z, at_y)
    inner, inner_at = (y, z), (at_y, at_z)
    pending = []

    def send(src, dst, sems, i, device):
        copy = pltpu.make_async_remote_copy(
            src_ref=src, dst_ref=dst, send_sem=sems.at[0, i], recv_sem=sems.at[1, i],
            device_id=device, device_id_type=MESH,
        )
        copy.start()
        pending.append(copy)
        return copy

    loads = []
    for i, (src, dst) in enumerate((
        (amp_in, amp), (slab_in, slab), (pairs_in, pairs), (virr_in, virr), (oirr_in, oirr),
        (venergy_in, venergy), (oenergy_in, oenergy), (integ, vraw),
    )):
        loads.append(pltpu.make_async_copy(src, dst, lsem.at[i]))
        loads[-1].start()
    barrier = pltpu.get_barrier_semaphore()
    for device in [f(d) for f in (at_x, at_y, at_z) for d in steps] + [other]:
        pl.semaphore_signal(barrier, inc=1, device_id=device, device_id_type=MESH)
    loads[1].wait()

    tiles = slab[...]
    c_of, d_of = tiles >> 4, tiles & 15
    pick = hot(iota((VIRT, TILES), 0) == jnp.where(d_of == v // 8, c_of, -1))
    found = own_slots(tiles, v)
    place = iota((1, TILES), 1).astype(F32)
    ids = [
        jnp.sum(jnp.where(place == k, tiles.astype(F32), 0.0), axis=1, keepdims=True) for k in found
    ]
    tile = by_slot(ids, (1, 128), 1).astype(I32)
    wide = iota((1, 128), 1) & 31
    pick_own = hot(iota((VIRT, 128), 0) == (tile & 15) * WIDTH + wide)
    loads[0].wait()
    block = amp[...].reshape(ROWS * A_DEV, VIRT)
    lane = iota((1, N * 128), 1)
    target = jnp.where((lane & 31) < PART, (lane >> 7) * PART + (lane & 31), -1)
    place_in = hot(iota((TILES, N * 128), 0) == target)
    row = iota((ROWS * A_DEV, 1), 0) & 3
    columns = dot(dot(block, pick).astype(BF), place_in)
    columns = jnp.where(row == ((lane >> 5) & 3), columns, 0.0).astype(BF)
    held = jnp.where(row == ((tile >> 4) & 3), dot(block, pick_own), 0.0).astype(BF)
    fold = hot((iota((ROWS, ROWS * A_DEV), 1) >> 2) == iota((ROWS, ROWS * A_DEV), 0))
    columns = dot(fold, columns).astype(BF)
    held = dot(fold, held).astype(BF)
    for o in range(N):
        xs[o, :, 0:128] = held
        xs[o, :, 128:256] = columns[:, o * 128 : (o + 1) * 128]
    pl.semaphore_wait(barrier, 3 * (N - 1) + 1)

    to_x = [send(xs.at[(x + d) % N], xa.at[x], xsem, d, at_x(d)) for d in FAR]
    xa[pl.ds(x, 1)] = xs[pl.ds(x, 1)]

    for i in range(2, 7):
        loads[i].wait()
    lists = pairs[...]
    first, second = lists[0:1, :], lists[1:2, :]
    code = first * 256 + second
    swapped = jnp.broadcast_to((second * 256 + first).astype(F32), (PAIRS, PAIRS)).T
    perm[...] = hot(swapped == code.astype(F32))
    part_lane = iota((1, DEPTH), 1)
    for h in range(2):
        holder = (y * N + z) * 2 + h
        slots = [k - (x * PART).astype(F32) for k in own_slots(tiles, holder)]
        r = iota((128, 1), 0)
        slot_at = by_slot(slots, (128, 1), 0).astype(I32)
        slot_at = jnp.where(r < 96, slot_at, -1)
        spread[h, 0:128] = hot(
            (slot_at == (part_lane >> 5)) & ((r & 31) == (part_lane & 31))
        )
        spread[h, 128:256] = hot(
            ((r & 31) == (part_lane >> 5))
            & ((holder % N) * A_DEV + (r >> 5) == (part_lane & 31))
        )
    irrep_hot = hot(iota((oirr.shape[1], PAIRS), 0) == first)
    irrep_hot2 = hot(iota((oirr.shape[1], PAIRS), 0) == second)
    occ = jnp.broadcast_to(oirr[...].astype(F32), (8, oirr.shape[1])).astype(BF)
    pair_sym = dot(occ, irrep_hot).astype(I32) ^ dot(occ, irrep_hot2).astype(I32)
    psb[...] = jnp.broadcast_to(pair_sym[0:1].astype(F32), (128, PAIRS)).T
    own_hot = hot(iota((TILES, DEPTH), 0) == x * PART + (part_lane >> 5))

    def own(row_values):
        wide_values = jnp.broadcast_to(row_values.astype(F32), (8, row_values.shape[1])).astype(BF)
        return dot(wide_values, own_hot)[0:1].astype(I32)

    c_row = own(c_of >> 2) * 4 + own(c_of & 3)
    d_row = own(d_of) * WIDTH + (part_lane & 31)
    vir = jnp.broadcast_to(virr[...].astype(F32), (8, VIRT)).astype(BF)
    tile_sym = [
        dot(vir, hot(iota((VIRT, DEPTH), 0) == rows))[0:1].astype(I32) for rows in (c_row, d_row)
    ]
    tsym[...] = jnp.broadcast_to((tile_sym[0] ^ tile_sym[1]).astype(F32), (8, DEPTH))

    ri, ci = iota((128, 128), 0), iota((128, 128), 1)
    regroup = hot(((ri >> 5) == (ci & 3)) & ((ri & 31) == (ci >> 2)))

    def relayout(k, _):
        rows = dot(regroup, vraw[k].reshape(WIDTH * A_DEV, VIRT)).astype(BF)
        at = pl.ds(pl.multiple_of(k * WIDTH, WIDTH), WIDTH)
        for a in range(A_DEV):
            vr[a, at, :] = rows[a * WIDTH : (a + 1) * WIDTH]
        return 0

    loads[7].wait()
    for copy in to_x:
        copy.wait_recv()

    to_core = [send(xa.at[pl.ds((1 - c) * 4, 4), :, 0:128], xoth.at[0], csem, 0, other)]
    columns = xa[:, :, 128:256].reshape(PAIRS, 128)

    def mirrored(half):
        at = pl.ds(pl.multiple_of(half * 128, 128), 128)
        return dot(perm[at, :], columns).astype(BF).reshape(4, ROWS, 128)

    xgive[...] = mirrored(1 - c)
    to_core.append(send(xgive, xoth.at[1], csem, 1, other))
    xmine[0] = xa[pl.ds(c * 4, 4), :, 0:128]
    xmine[1] = mirrored(c)

    def spread_out(ref, h):
        rows = jnp.concatenate([ref[i].reshape(128, 128) for i in range(2)], axis=1)
        return dot(rows, spread[h])

    dense = spread_out(xmine, c)
    for copy in to_core:
        copy.wait_recv()
    dense += spread_out(xoth, 1 - c)
    for p in range(2):
        ps[p] = dense[:, p * PATH : (p + 1) * PATH].astype(BF).reshape(N, PIECE, PATH)
    copies = [
        send(ps.at[p, (outer[p] + d) % N], pr.at[p, outer[p]], psem.at[p], d, outer_at[p](d))
        for d in FAR for p in range(2)
    ]
    for p in range(2):
        pr[p, pl.ds(outer[p], 1)] = ps[p, pl.ds(outer[p], 1)]
    lax.fori_loop(0, 8, relayout, 0)
    for copy in copies:
        copy.wait_recv()
    for p in range(2):
        total = pr[p, 0].astype(F32)
        for i in steps:
            total += pr[p, i].astype(F32)
        qs[p] = total.astype(BF)
    copies = [
        send(qs.at[p], qr.at[p, inner[p]], qsem.at[p], d, inner_at[p](d))
        for d in FAR for p in range(2)
    ]
    for p in range(2):
        qr[p, pl.ds(inner[p], 1)] = qs[p].reshape(1, PIECE, PATH)
    lax.fori_loop(8, 16, relayout, 0)
    for copy in copies:
        copy.wait_recv()
    mine = [c * N + outer[p] for p in range(2)]
    for p in range(2):
        total = qr[p, 0].astype(F32)
        for i in steps:
            total += qr[p, i].astype(F32)
        sym_of = psb[pl.ds(pl.multiple_of(mine[p] * PIECE, PIECE), PIECE), :][:, 0:1]
        total = jnp.where(sym_of == tsym[0:1, p * PATH : (p + 1) * PATH], total, 0.0)
        sy[p, pl.ds(mine[p], 1)] = total.astype(BF).reshape(1, PIECE, PATH)
    gathered = {
        (p, d): send(sy.at[p, mine[p]], sy.at[p, mine[p]], gsem.at[p], d, outer_at[p](d))
        for d in FAR for p in range(2)
    }
    to_other = [
        send(sy.at[p, mine[p]], sy.at[p, mine[p]], hsem.at[p], 0, other) for p in range(2)
    ]
    lax.fori_loop(16, 24, relayout, 0)
    for d in NEAR:
        for p in range(2):
            gathered[p, d].wait_recv()
            got = c * N + (outer[p] + N - d) % N
            to_other.append(send(sy.at[p, got], sy.at[p, got], hsem.at[p], d, other))
    for copy in to_other:
        copy.wait_recv()

    ring = {}

    def pass_on(way, i, q, got):
        distance = 4 - i if i < 4 else 7 - i
        d = distance if way == 0 else N - distance
        half = 0 if (way == 0) == (i < 4) else PIECE
        value = pf[d, half : half + PIECE, q * VIRT : (q + 1) * VIRT]
        if got is not None:
            value += rr[way, got, q].astype(F32)
        rs[way, i, q] = value.astype(BF)
        ring[way, i, q] = send(
            rs.at[way, i, q], rr.at[way, i, q], rsem.at[way, q], i, at_x(1 if way == 0 else N - 1)
        )

    def multiply(blocks, first):
        rows = jnp.concatenate(
            [
                jnp.concatenate(
                    [sy[p, pl.ds(((x + d) % N) * 2, 2)].reshape(ROWS, PATH) for p in range(2)],
                    axis=1,
                )
                for d in blocks
            ],
            axis=0,
        )
        for a in range(A_DEV):
            sums = dot(rows, vr[a])
            for i, d in enumerate(blocks):
                pf[d, :, a * VIRT : (a + 1) * VIRT] = sums[i * ROWS : (i + 1) * ROWS]
            if first:
                for i in (0, 4):
                    for way in range(2):
                        pass_on(way, i, a, None)

    multiply((4, 3, 5, 2), True)
    multiply((6, 1, 7, 0), False)
    occ = jnp.broadcast_to(oenergy[...], (8, oirr.shape[1]))
    energy = sum(
        jnp.dot(
            occ, jnp.where(iota((oirr.shape[1], PAIRS), 0) == which, 1.0, 0.0),
            precision=lax.Precision.HIGHEST, preferred_element_type=F32,
        )
        for which in (first, second)
    )
    turned = jnp.broadcast_to(energy[0:1], (128, PAIRS)).T
    inverse[:, 0:128] = turned[0:ROWS]
    for o in steps:
        inverse[:, 0:128] = jnp.where(x == o, turned[o * ROWS : (o + 1) * ROWS], inverse[:, 0:128])
    pair_energy = inverse[:, 0:1]
    vir_row = venergy[...]
    vir_lane = iota((1, VIRT), 1)
    for a in range(A_DEV):
        own_virtual = jnp.sum(
            jnp.where(vir_lane == v * A_DEV + a, vir_row, 0.0), axis=1, keepdims=True
        )
        inverse[:, a * VIRT : (a + 1) * VIRT] = 1.0 / (pair_energy - own_virtual - vir_row)
    for i in (0, 4, 1, 5, 2):
        for q in range(4):
            for way in range(2):
                ring[way, i, q].wait_recv()
                pass_on(way, i + 1, q, i)
    for q in range(4):
        for i in (6, 3):
            for way in range(2):
                ring[way, i, q].wait_recv()
        for half, mine_, theirs in ((0, 3, 6), (PIECE, 6, 3)):
            at = (slice(half, half + PIECE), slice(q * VIRT, (q + 1) * VIRT))
            total = pf[0, at[0], at[1]] + rr[0, mine_, q].astype(F32) + rr[1, theirs, q].astype(F32)
            total = total * inverse[at[0], at[1]]
            out[at[0], q, :] = total.astype(out.dtype)
    for copy in pending:
        copy.wait_send()


def local(
    amplitudes, integrals, pair_list, slab_tiles, occ_irrep, vir_irrep, occ_energy, vir_energy
):
    dma = pltpu.SemaphoreType.DMA
    occupied = occ_irrep.shape[0]
    return pl.pallas_call(
        kernel,
        out_shape=jax.ShapeDtypeStruct((ROWS, A_DEV, VIRT), BF),
        in_specs=[pl.BlockSpec(memory_space=pl.ANY)] * 8,
        out_specs=pl.BlockSpec(memory_space=pltpu.VMEM),
        scratch_shapes=[
            pltpu.VMEM((ROWS, A_DEV, VIRT), BF),
            pltpu.VMEM((1, TILES), I32),
            pltpu.VMEM((2, PAIRS), I32),
            pltpu.VMEM((1, VIRT), I32),
            pltpu.VMEM((1, occupied), I32),
            pltpu.VMEM((1, VIRT), F32),
            pltpu.VMEM((1, occupied), F32),
            pltpu.VMEM((PART, WIDTH, A_DEV, VIRT), BF),
            pltpu.VMEM((A_DEV, DEPTH, VIRT), BF),
            pltpu.VMEM((N, ROWS, 256), BF),
            pltpu.VMEM((N, ROWS, 256), BF),
            pltpu.VMEM((PAIRS, PAIRS), BF),
            pltpu.VMEM((2, 256, DEPTH), BF),
            pltpu.VMEM((PAIRS, 128), F32),
            pltpu.VMEM((8, DEPTH), F32),
            pltpu.VMEM((ROWS, COLS), F32),
            pltpu.VMEM((2, 4, ROWS, 128), BF),
            pltpu.VMEM((4, ROWS, 128), BF),
            pltpu.VMEM((2, 4, ROWS, 128), BF),
            pltpu.VMEM((2, N, PIECE, PATH), BF),
            pltpu.VMEM((2, N, PIECE, PATH), BF),
            pltpu.VMEM((2, PIECE, PATH), BF),
            pltpu.VMEM((2, N, PIECE, PATH), BF),
            pltpu.VMEM((2, 2 * N, PIECE, PATH), BF),
            pltpu.VMEM((N, ROWS, COLS), F32),
            pltpu.VMEM((2, 7, 4, PIECE, VIRT), BF),
            pltpu.VMEM((2, 7, 4, PIECE, VIRT), BF),
            dma((8,)),
            dma((2, N)),
            dma((2, 2)),
            dma((2, 2, N)),
            dma((2, 2, N)),
            dma((2, 2, N)),
            dma((2, 2, N)),
            dma((2, 4, 2, 7)),
        ],
        compiler_params=pltpu.CompilerParams(
            collective_id=0, has_side_effects=True, vmem_limit_bytes=60 << 20
        ),
    )(
        amplitudes,
        integrals,
        slab_tiles.reshape(1, TILES),
        pair_list.T,
        vir_irrep.reshape(1, VIRT),
        occ_irrep.reshape(1, occupied),
        vir_energy.reshape(1, VIRT),
        occ_energy.reshape(1, occupied),
    )


def solution(mesh):
    in_specs = (
        P("opair", "vpair", None), P("opair", None, "vpair", None), P(), P(), P(), P(), P(), P(),
    )
    out_specs = P("opair", "vpair", None)
    return jax.shard_map(local, mesh=mesh, in_specs=in_specs, out_specs=out_specs, check_vma=False)
```

```python
import jax
import jax.numpy as jnp
from jax import lax
from jax.experimental import pallas as pl
from jax.experimental.pallas import tpu as pltpu
from jax.sharding import PartitionSpec as P

MESH = pl.DeviceIdType.MESH
BF = jnp.bfloat16
F32 = jnp.float32
I32 = jnp.int32
N = 8
PAIRS, ROWS, PIECE = 256, 32, 16
TILES, PART, WIDTH = 192, 24, 32
A_DEV, VIRT = 4, 512
DEPTH = PART * WIDTH
COLS = A_DEV * VIRT
PATH = DEPTH // 2
FAR = (4, 3, 5, 2, 6, 1, 7)
NEAR = (1, 7, 2, 6, 3, 5, 4)


def iota(shape, axis):
    return lax.broadcasted_iota(I32, shape, axis)


def hot(mask):
    return jnp.where(mask, 1.0, 0.0).astype(BF)


def dot(a, b):
    return jnp.dot(a, b, preferred_element_type=F32)


def own_slots(tiles, owner):
    place = iota((1, TILES), 1).astype(F32)
    held = (tiles >> 6) == owner
    found, last = [], None
    for _ in range(3):
        open_ = held if last is None else held & (place > last)
        last = jnp.min(jnp.where(open_, place, 999.0), axis=1, keepdims=True)
        found.append(last)
    return found


def by_slot(values, shape, axis):
    slot = iota(shape, axis) >> 5
    return jnp.where(slot == 0, values[0], jnp.where(slot == 1, values[1], values[2]))


def kernel(
    amp_in, integ, slab_in, pairs_in, virr_in, oirr_in, venergy_in, oenergy_in, out,
    amp, slab, pairs, virr, oirr, venergy, oenergy,
    vraw, vr, xs, xa, perm, spread, psb, tsym, inverse, xmine, xgive, xoth,
    ps, pr, qs, qr, sy, pf, rs, rr,
    lsem, xsem, csem, psem, qsem, gsem, hsem, rsem,
):
    v = lax.axis_index("vpair")
    x = lax.axis_index("opair")
    y, z, c = v // 16, (v // 2) % N, v % 2

    def at_x(d):
        return {"vpair": v, "opair": (x + d) % N}

    def at_y(d):
        return {"vpair": (((y + d) % N) * N + z) * 2 + c, "opair": x}

    def at_z(d):
        return {"vpair": (y * N + (z + d) % N) * 2 + c, "opair": x}

    other = {"vpair": (y * N + z) * 2 + (1 - c), "opair": x}
    steps = range(1, N)
    outer, outer_at = (z, y), (at_z, at_y)
    inner, inner_at = (y, z), (at_y, at_z)
    pending = []

    def send(src, dst, sems, i, device):
        copy = pltpu.make_async_remote_copy(
            src_ref=src, dst_ref=dst, send_sem=sems.at[0, i], recv_sem=sems.at[1, i],
            device_id=device, device_id_type=MESH,
        )
        copy.start()
        pending.append(copy)
        return copy

    loads = []
    for i, (src, dst) in enumerate((
        (amp_in, amp), (slab_in, slab), (pairs_in, pairs), (virr_in, virr), (oirr_in, oirr),
        (venergy_in, venergy), (oenergy_in, oenergy), (integ, vraw),
    )):
        loads.append(pltpu.make_async_copy(src, dst, lsem.at[i]))
        loads[-1].start()
    barrier = pltpu.get_barrier_semaphore()
    for device in [f(d) for f in (at_x, at_y, at_z) for d in steps] + [other]:
        pl.semaphore_signal(barrier, inc=1, device_id=device, device_id_type=MESH)
    loads[1].wait()

    tiles = slab[...]
    c_of, d_of = tiles >> 4, tiles & 15
    pick = hot(iota((VIRT, TILES), 0) == jnp.where(d_of == v // 8, c_of, -1))
    found = own_slots(tiles, v)
    place = iota((1, TILES), 1).astype(F32)
    ids = [
        jnp.sum(jnp.where(place == k, tiles.astype(F32), 0.0), axis=1, keepdims=True) for k in found
    ]
    tile = by_slot(ids, (1, 128), 1).astype(I32)
    wide = iota((1, 128), 1) & 31
    pick_own = hot(iota((VIRT, 128), 0) == (tile & 15) * WIDTH + wide)
    loads[0].wait()
    block = amp[...].reshape(ROWS * A_DEV, VIRT)
    lane = iota((1, N * 128), 1)
    target = jnp.where((lane & 31) < PART, (lane >> 7) * PART + (lane & 31), -1)
    place_in = hot(iota((TILES, N * 128), 0) == target)
    row = iota((ROWS * A_DEV, 1), 0) & 3
    columns = dot(dot(block, pick).astype(BF), place_in)
    columns = jnp.where(row == ((lane >> 5) & 3), columns, 0.0).astype(BF)
    held = jnp.where(row == ((tile >> 4) & 3), dot(block, pick_own), 0.0).astype(BF)
    fold = hot((iota((ROWS, ROWS * A_DEV), 1) >> 2) == iota((ROWS, ROWS * A_DEV), 0))
    columns = dot(fold, columns).astype(BF)
    held = dot(fold, held).astype(BF)
    for o in range(N):
        xs[o, :, 0:128] = held
        xs[o, :, 128:256] = columns[:, o * 128 : (o + 1) * 128]
    pl.semaphore_wait(barrier, 3 * (N - 1) + 1)

    to_x = [send(xs.at[(x + d) % N], xa.at[x], xsem, d, at_x(d)) for d in FAR]
    xa[pl.ds(x, 1)] = xs[pl.ds(x, 1)]

    for i in range(2, 7):
        loads[i].wait()
    lists = pairs[...]
    first, second = lists[0:1, :], lists[1:2, :]
    code = first * 256 + second
    swapped = jnp.broadcast_to((second * 256 + first).astype(F32), (PAIRS, PAIRS)).T
    perm[...] = hot(swapped == code.astype(F32))
    part_lane = iota((1, DEPTH), 1)
    for h in range(2):
        holder = (y * N + z) * 2 + h
        slots = [k - (x * PART).astype(F32) for k in own_slots(tiles, holder)]
        r = iota((128, 1), 0)
        slot_at = by_slot(slots, (128, 1), 0).astype(I32)
        slot_at = jnp.where(r < 96, slot_at, -1)
        spread[h, 0:128] = hot(
            (slot_at == (part_lane >> 5)) & ((r & 31) == (part_lane & 31))
        )
        spread[h, 128:256] = hot(
            ((r & 31) == (part_lane >> 5))
            & ((holder % N) * A_DEV + (r >> 5) == (part_lane & 31))
        )
    irrep_hot = hot(iota((oirr.shape[1], PAIRS), 0) == first)
    irrep_hot2 = hot(iota((oirr.shape[1], PAIRS), 0) == second)
    occ = jnp.broadcast_to(oirr[...].astype(F32), (8, oirr.shape[1])).astype(BF)
    pair_sym = dot(occ, irrep_hot).astype(I32) ^ dot(occ, irrep_hot2).astype(I32)
    psb[...] = jnp.broadcast_to(pair_sym[0:1].astype(F32), (128, PAIRS)).T
    own_hot = hot(iota((TILES, DEPTH), 0) == x * PART + (part_lane >> 5))

    def own(row_values):
        wide_values = jnp.broadcast_to(row_values.astype(F32), (8, row_values.shape[1])).astype(BF)
        return dot(wide_values, own_hot)[0:1].astype(I32)

    c_row = own(c_of >> 2) * 4 + own(c_of & 3)
    d_row = own(d_of) * WIDTH + (part_lane & 31)
    vir = jnp.broadcast_to(virr[...].astype(F32), (8, VIRT)).astype(BF)
    tile_sym = [
        dot(vir, hot(iota((VIRT, DEPTH), 0) == rows))[0:1].astype(I32) for rows in (c_row, d_row)
    ]
    tsym[...] = jnp.broadcast_to((tile_sym[0] ^ tile_sym[1]).astype(F32), (8, DEPTH))

    ri, ci = iota((128, 128), 0), iota((128, 128), 1)
    regroup = hot(((ri >> 5) == (ci & 3)) & ((ri & 31) == (ci >> 2)))

    def relayout(k, _):
        rows = dot(regroup, vraw[k].reshape(WIDTH * A_DEV, VIRT)).astype(BF)
        at = pl.ds(pl.multiple_of(k * WIDTH, WIDTH), WIDTH)
        for a in range(A_DEV):
            vr[a, at, :] = rows[a * WIDTH : (a + 1) * WIDTH]
        return 0

    loads[7].wait()
    for copy in to_x:
        copy.wait_recv()

    to_core = [send(xa.at[pl.ds((1 - c) * 4, 4), :, 0:128], xoth.at[0], csem, 0, other)]
    columns = xa[:, :, 128:256].reshape(PAIRS, 128)

    def mirrored(half):
        at = pl.ds(pl.multiple_of(half * 128, 128), 128)
        return dot(perm[at, :], columns).astype(BF).reshape(4, ROWS, 128)

    xgive[...] = mirrored(1 - c)
    to_core.append(send(xgive, xoth.at[1], csem, 1, other))
    xmine[0] = xa[pl.ds(c * 4, 4), :, 0:128]
    xmine[1] = mirrored(c)

    def spread_out(ref, h):
        rows = jnp.concatenate([ref[i].reshape(128, 128) for i in range(2)], axis=1)
        return dot(rows, spread[h])

    dense = spread_out(xmine, c)
    for copy in to_core:
        copy.wait_recv()
    dense += spread_out(xoth, 1 - c)
    for p in range(2):
        ps[p] = dense[:, p * PATH : (p + 1) * PATH].astype(BF).reshape(N, PIECE, PATH)
    copies = [
        send(ps.at[p, (outer[p] + d) % N], pr.at[p, outer[p]], psem.at[p], d, outer_at[p](d))
        for d in FAR for p in range(2)
    ]
    for p in range(2):
        pr[p, pl.ds(outer[p], 1)] = ps[p, pl.ds(outer[p], 1)]
    lax.fori_loop(0, 10, relayout, 0)
    occ = jnp.broadcast_to(oenergy[...], (8, oirr.shape[1]))
    energy = sum(
        jnp.dot(
            occ, jnp.where(iota((oirr.shape[1], PAIRS), 0) == which, 1.0, 0.0),
            precision=lax.Precision.HIGHEST, preferred_element_type=F32,
        )
        for which in (first, second)
    )
    turned = jnp.broadcast_to(energy[0:1], (128, PAIRS)).T
    inverse[:, 0:128] = turned[0:ROWS]
    for o in steps:
        inverse[:, 0:128] = jnp.where(x == o, turned[o * ROWS : (o + 1) * ROWS], inverse[:, 0:128])
    pair_energy = inverse[:, 0:1]
    vir_row = venergy[...]
    vir_lane = iota((1, VIRT), 1)
    for a in range(A_DEV):
        own_virtual = jnp.sum(
            jnp.where(vir_lane == v * A_DEV + a, vir_row, 0.0), axis=1, keepdims=True
        )
        inverse[:, a * VIRT : (a + 1) * VIRT] = 1.0 / (pair_energy - own_virtual - vir_row)
    for copy in copies:
        copy.wait_recv()
    for p in range(2):
        total = pr[p, 0].astype(F32)
        for i in steps:
            total += pr[p, i].astype(F32)
        qs[p] = total.astype(BF)
    copies = [
        send(qs.at[p], qr.at[p, inner[p]], qsem.at[p], d, inner_at[p](d))
        for d in FAR for p in range(2)
    ]
    for p in range(2):
        qr[p, pl.ds(inner[p], 1)] = qs[p].reshape(1, PIECE, PATH)
    lax.fori_loop(10, 24, relayout, 0)
    for copy in copies:
        copy.wait_recv()
    mine = [c * N + outer[p] for p in range(2)]
    for p in range(2):
        total = qr[p, 0].astype(F32)
        for i in steps:
            total += qr[p, i].astype(F32)
        sym_of = psb[pl.ds(pl.multiple_of(mine[p] * PIECE, PIECE), PIECE), :][:, 0:1]
        total = jnp.where(sym_of == tsym[0:1, p * PATH : (p + 1) * PATH], total, 0.0)
        sy[p, pl.ds(mine[p], 1)] = total.astype(BF).reshape(1, PIECE, PATH)
    gathered = {
        (p, d): send(sy.at[p, mine[p]], sy.at[p, mine[p]], gsem.at[p], d, outer_at[p](d))
        for d in FAR for p in range(2)
    }
    half = pl.ds(c * N, N)
    to_other = []
    for p in range(2):
        for d in NEAR:
            gathered[p, d].wait_recv()
        to_other.append(send(sy.at[p, half], sy.at[p, half], hsem, p, other))
    for copy in to_other:
        copy.wait_recv()

    ring = {}

    def pass_on(way, i, q, got):
        distance = 4 - i if i < 4 else 7 - i
        d = distance if way == 0 else N - distance
        half = 0 if (way == 0) == (i < 4) else PIECE
        value = pf[d, half : half + PIECE, q * VIRT : (q + 1) * VIRT]
        if got is not None:
            value += rr[way, got, q].astype(F32)
        rs[way, i, q] = value.astype(BF)
        ring[way, i, q] = send(
            rs.at[way, i, q], rr.at[way, i, q], rsem.at[way, q], i, at_x(1 if way == 0 else N - 1)
        )

    def multiply(blocks):
        rows = jnp.concatenate(
            [
                jnp.concatenate(
                    [sy[p, pl.ds(((x + d) % N) * 2, 2)].reshape(ROWS, PATH) for p in range(2)],
                    axis=1,
                )
                for d in blocks
            ],
            axis=0,
        )
        for a in range(A_DEV):
            sums = dot(rows, vr[a])
            for i, d in enumerate(blocks):
                pf[d, :, a * VIRT : (a + 1) * VIRT] = sums[i * ROWS : (i + 1) * ROWS]
            for i in (0, 4):
                for way in range(2):
                    pass_on(way, i, a, None)

    multiply((4, 3, 5, 2, 6, 1, 7, 0))
    for i in (0, 4, 1, 5, 2):
        for q in range(4):
            for way in range(2):
                ring[way, i, q].wait_recv()
                pass_on(way, i + 1, q, i)
    for q in range(4):
        for i in (6, 3):
            for way in range(2):
                ring[way, i, q].wait_recv()
        for half, mine_, theirs in ((0, 3, 6), (PIECE, 6, 3)):
            at = (slice(half, half + PIECE), slice(q * VIRT, (q + 1) * VIRT))
            total = pf[0, at[0], at[1]] + rr[0, mine_, q].astype(F32) + rr[1, theirs, q].astype(F32)
            total = total * inverse[at[0], at[1]]
            out[at[0], q, :] = total.astype(out.dtype)
    for copy in pending:
        copy.wait_send()


def local(
    amplitudes, integrals, pair_list, slab_tiles, occ_irrep, vir_irrep, occ_energy, vir_energy
):
    dma = pltpu.SemaphoreType.DMA
    occupied = occ_irrep.shape[0]
    return pl.pallas_call(
        kernel,
        out_shape=jax.ShapeDtypeStruct((ROWS, A_DEV, VIRT), BF),
        in_specs=[pl.BlockSpec(memory_space=pl.ANY)] * 8,
        out_specs=pl.BlockSpec(memory_space=pltpu.VMEM),
        scratch_shapes=[
            pltpu.VMEM((ROWS, A_DEV, VIRT), BF),
            pltpu.VMEM((1, TILES), I32),
            pltpu.VMEM((2, PAIRS), I32),
            pltpu.VMEM((1, VIRT), I32),
            pltpu.VMEM((1, occupied), I32),
            pltpu.VMEM((1, VIRT), F32),
            pltpu.VMEM((1, occupied), F32),
            pltpu.VMEM((PART, WIDTH, A_DEV, VIRT), BF),
            pltpu.VMEM((A_DEV, DEPTH, VIRT), BF),
            pltpu.VMEM((N, ROWS, 256), BF),
            pltpu.VMEM((N, ROWS, 256), BF),
            pltpu.VMEM((PAIRS, PAIRS), BF),
            pltpu.VMEM((2, 256, DEPTH), BF),
            pltpu.VMEM((PAIRS, 128), F32),
            pltpu.VMEM((8, DEPTH), F32),
            pltpu.VMEM((ROWS, COLS), F32),
            pltpu.VMEM((2, 4, ROWS, 128), BF),
            pltpu.VMEM((4, ROWS, 128), BF),
            pltpu.VMEM((2, 4, ROWS, 128), BF),
            pltpu.VMEM((2, N, PIECE, PATH), BF),
            pltpu.VMEM((2, N, PIECE, PATH), BF),
            pltpu.VMEM((2, PIECE, PATH), BF),
            pltpu.VMEM((2, N, PIECE, PATH), BF),
            pltpu.VMEM((2, 2 * N, PIECE, PATH), BF),
            pltpu.VMEM((N, ROWS, COLS), F32),
            pltpu.VMEM((2, 7, 4, PIECE, VIRT), BF),
            pltpu.VMEM((2, 7, 4, PIECE, VIRT), BF),
            dma((8,)),
            dma((2, N)),
            dma((2, 2)),
            dma((2, 2, N)),
            dma((2, 2, N)),
            dma((2, 2, N)),
            dma((2, 2)),
            dma((2, 4, 2, 7)),
        ],
        compiler_params=pltpu.CompilerParams(
            collective_id=0, has_side_effects=True, vmem_limit_bytes=60 << 20
        ),
    )(
        amplitudes,
        integrals,
        slab_tiles.reshape(1, TILES),
        pair_list.T,
        vir_irrep.reshape(1, VIRT),
        occ_irrep.reshape(1, occupied),
        vir_energy.reshape(1, VIRT),
        occ_energy.reshape(1, occupied),
    )


def solution(mesh):
    in_specs = (
        P("opair", "vpair", None), P("opair", None, "vpair", None), P(), P(), P(), P(), P(), P(),
    )
    out_specs = P("opair", "vpair", None)
    return jax.shard_map(local, mesh=mesh, in_specs=in_specs, out_specs=out_specs, check_vma=False)
```
